256 devices in a mesh: vgroup: 8 (over x, core), feat: 32 (over z, y).
Axes of the slice: x: 4, y: 4, z: 8, core: 2. Of those that a mesh axis runs over, the one named last changes fastest.
Arguments:
- features_t: bfloat16 [8, 1024, 32768], P('vgroup', 'feat'), may hold values from -6 to 6
- tile_weights: bfloat16 [8, 1024, 128, 128], P('vgroup'), may hold values from -0.1875 to 0.1875
- tile_dst: int32 [8, 1024], P('vgroup'), may hold values from 0 to 127
- tile_src: int32 [8, 1024], P('vgroup'), may hold values from 0 to 255
- tile_count: int32 [8], P('vgroup'), may hold values from 256 to 1024, as said below
- w_self: bfloat16 [1024, 256], P('feat'), may hold values from -0.1875 to 0.1875
- w_neigh: bfloat16 [1024, 256], P('feat'), may hold values from -0.1875 to 0.1875
- bias: float32 [256], replicated, may hold values from -4 to 4
- grad_hidden: bfloat16 [131072, 256], P(('vgroup', 'feat')), may hold values from -1 to 1
Outputs:
- hidden: bfloat16 [131072, 256], P(('vgroup', 'feat'))
- grad_self: float32 [1024, 256], P('feat')
- grad_neigh: float32 [1024, 256], P('feat')
- grad_bias: float32 [256], replicated
The draws below stay inside these ranges and needn't reach their ends.
Inputs may be any that keep to these rules, and one draw needn't show every extreme that they name: `tile_count`: slots at or past a group's count are ignored; at least one group has all 1024 slots live.
All inputs are finite; a program needn't handle non-finite values.
Results may differ from the reference program's by a relative error of at most 0.0075.
Values may be sent and summed in bfloat16 or wider, within the bound.
No kernel may reach another device: no remote copies, remote signals or barrier semaphores. Data moves between devices by JAX's collectives and lax.ppermute only.
A program may use at most 192 MiB of HBM per device.

```python
import jax
import jax.numpy as jnp
from jax import lax

F = 1024
H = 256
TILE = 128
TPR = 8
GROUPS = 8
NDST = 16384
DT = 128
ST = 256
NSRC = 32768
TILES = 1024
ROWS = 131072


def draw_tile_count(key, part):
    base = jax.random.fold_in(key, 11)
    first_key, second_key = jax.random.split(base)
    counts = jax.random.randint(first_key, (GROUPS,), TILES // 4, TILES + 1)
    full_group = jax.random.randint(second_key, (), 0, GROUPS)
    return jnp.where(jnp.arange(GROUPS) == full_group, TILES, counts).astype(jnp.int32)


def set_ends(values, stream_key, smallest, largest):
    longest = values.shape.index(max(values.shape))
    spots = []
    for shift in (0, 1):
        where = [jax.random.randint(jax.random.fold_in(stream_key, axis), (), 0, length) for axis, length in enumerate(values.shape)]
        where[longest] = (where[longest] + shift) % values.shape[longest]
        spots.append(tuple(where))
    return values.at[spots[0]].set(smallest).at[spots[1]].set(largest)


def block_scale(stream_key, dims, shards, smallest, top_value):
    factor_of = 1.0
    for dim, shards_of in shards:
        heights = jax.random.uniform(jax.random.fold_in(jax.random.fold_in(stream_key, 6), dim), (shards_of,), jnp.float32, smallest / len(shards), top_value / len(shards))
        factor_of = factor_of * jnp.repeat(jnp.exp(heights), dims[dim] // shards_of).reshape((-1,) + (1,) * (len(dims) - 1 - dim))
    return factor_of


def noise(own_key, dims, spread, reach, cuts=(), kind=jnp.bfloat16):
    values = jax.random.normal(own_key, dims, jnp.float32) * spread
    if len(cuts) > 0:
        values = block_scale(own_key, dims, cuts, -0.22, 0.18) * values
    return jnp.clip(values, min=-reach, max=reach).astype(kind)


def setup_inputs(seed: int = 0) -> dict:
    key_list = jax.random.split(jax.random.key(seed), 10)
    return {
        "features_t": noise(key_list[0], (GROUPS, F, NSRC), 1.0, 6.0, ((0, 8), (1, 32))),
        "tile_weights": noise(key_list[1], (GROUPS, TILES, TILE, TILE), (TPR * TILE) ** -0.5, 0.1875, ((0, 8),)),
        "tile_dst": set_ends(jax.random.randint(key_list[2], (GROUPS, TILES), 0, DT), jax.random.fold_in(key_list[2], 1), 0, DT - 1).astype(jnp.int32),
        "tile_src": set_ends(jax.random.randint(key_list[3], (GROUPS, TILES), 0, ST), jax.random.fold_in(key_list[3], 1), 0, ST - 1).astype(jnp.int32),
        "tile_count": draw_tile_count(jax.random.fold_in(key_list[9], 71), 0),
        "w_self": noise(key_list[5], (F, H), F ** -0.5, 0.1875, ((0, 32),)),
        "w_neigh": noise(key_list[6], (F, H), F ** -0.5, 0.1875, ((0, 32),)),
        "bias": noise(key_list[7], (H,), 1.0, 4.0, (), jnp.float32),
        "grad_hidden": noise(key_list[8], (ROWS, H), 0.0625, 1.0, ((0, 256),)),
    }


def activate(pre):
    return jax.nn.gelu(pre, approximate=True)

def reference(features_t, tile_weights, tile_dst, tile_src, tile_count, w_self, w_neigh, bias, grad_hidden):
    upstream_all = grad_hidden.reshape(GROUPS, NDST, H)

    def one_group(items):
        feats, weights, dsts, srcs, count, upstream = items
        blocks = feats.reshape(F, ST, TILE)[:, srcs, :]
        product = jnp.einsum('ftk,tjk->ftj', blocks.astype(jnp.float32), weights.astype(jnp.float32))
        live = (jnp.arange(TILES) < count).astype(jnp.float32)
        onehot = (dsts[None, :] == jnp.arange(DT)[:, None]).astype(jnp.float32) * live[None, :]
        summed = jnp.einsum('dt,ftj->fdj', onehot, product, precision=lax.Precision.HIGHEST)
        aggregated = summed.reshape(F, NDST).astype(jnp.bfloat16)
        target_columns = feats[:, :NDST]
        pre = jnp.dot(target_columns.T, w_self, preferred_element_type=jnp.float32)
        pre = pre + jnp.dot(aggregated.T, w_neigh, preferred_element_type=jnp.float32) + bias
        output, pullback = jax.vjp(activate, pre)
        delta = pullback(upstream.astype(jnp.float32))[0].astype(jnp.bfloat16)
        grad_s = jnp.dot(target_columns, delta, preferred_element_type=jnp.float32)
        grad_n = jnp.dot(aggregated, delta, preferred_element_type=jnp.float32)
        grad_b = lax.optimization_barrier(jnp.sum(delta.astype(jnp.float32), axis=0))
        return (output.astype(jnp.bfloat16), grad_s, grad_n, grad_b)
    hidden, grad_s, grad_n, grad_b = lax.map(one_group, (features_t, tile_weights, tile_dst, tile_src, tile_count, upstream_all))
    return (hidden.reshape(GROUPS * NDST, H), lax.optimization_barrier(jnp.sum(grad_s, axis=0)), lax.optimization_barrier(jnp.sum(grad_n, axis=0)), lax.optimization_barrier(jnp.sum(grad_b, axis=0)))
```

```python
import jax
import jax.numpy as jnp
from jax import lax
from jax.experimental import pallas as pl
from jax.experimental.pallas import tpu as pltpu
from jax.sharding import PartitionSpec as P

TILE = 128
SLOTS_STEP = 128
UNROLL = 32
GELU_A = 0.7978845608
GELU_B = 0.044715
BF16 = jnp.bfloat16
F32 = jnp.float32


def aggregate(dsts, srcs, count, feats, weights, nfeat):
    fcols, nsrc = feats.shape
    slots = weights.shape[0]
    dtiles = nsrc // TILE // 2
    per_owner = dtiles // nfeat
    steps = slots // SLOTS_STEP

    def kernel(dst, src, cnt, x_ref, w_ref, o_ref, acc):
        i = pl.program_id(0)

        @pl.when(i == 0)
        def _():
            acc[...] = jnp.zeros_like(acc)

        base = i * SLOTS_STEP
        live = jnp.clip(cnt[0] - base, 0, SLOTS_STEP)
        zero = jnp.zeros((fcols, TILE), BF16)

        def source(slot):
            return x_ref[:, pl.ds(pl.multiple_of(src[slot] * TILE, TILE), TILE)]

        def group(g, carry):
            first = g * UNROLL
            products = []
            for u in range(0, UNROLL, 2):
                slot = base + first + u
                left = jnp.concatenate(
                    [
                        jnp.concatenate([source(slot), zero], 1),
                        jnp.concatenate([zero, source(slot + 1)], 1),
                    ],
                    0,
                )
                right = jnp.concatenate([w_ref[first + u], w_ref[first + u + 1]], 1)
                both = lax.dot_general(
                    left, right, (((1,), (1,)), ((), ())), preferred_element_type=F32
                )
                products += [both[:fcols], both[fcols:]]
            for u in range(UNROLL):
                slot = base + first + u
                acc[dst[slot]] += jnp.where(slot < cnt[0], products[u], 0.0)
            return carry

        lax.fori_loop(0, pl.cdiv(live, UNROLL), group, 0)

        @pl.when(i == steps - 1)
        def _():
            for c in range(nfeat):
                for q in range(per_owner):
                    o_ref[c, :, q * TILE : (q + 1) * TILE] = acc[c * per_owner + q].astype(BF16)

    return pl.pallas_call(
        kernel,
        grid_spec=pltpu.PrefetchScalarGridSpec(
            num_scalar_prefetch=3,
            grid=(steps,),
            in_specs=[
                pl.BlockSpec((fcols, nsrc), lambda i, *_: (0, 0)),
                pl.BlockSpec((SLOTS_STEP, TILE, TILE), lambda i, *_: (i, 0, 0)),
            ],
            out_specs=pl.BlockSpec((nfeat, fcols, per_owner * TILE), lambda i, *_: (0, 0, 0)),
            scratch_shapes=[pltpu.VMEM((dtiles, fcols, TILE), F32)],
        ),
        out_shape=jax.ShapeDtypeStruct((nfeat, fcols, per_owner * TILE), BF16),
        name="aggregate",
        compiler_params=pltpu.CompilerParams(vmem_limit_bytes=40 << 20),
        cost_estimate=pl.CostEstimate(
            flops=2 * slots * fcols * TILE * TILE,
            bytes_accessed=slots * TILE * TILE * 2 + fcols * nsrc * 2,
            transcendentals=0,
        ),
    )(dsts, srcs, count, feats, weights)


def contract_rows(a, b):
    return lax.dot_general(a, b, (((0,), (0,)), ((), ())), preferred_element_type=F32)


def own_part(place, w_rel, x_rows, bias):
    ny, nv, two_f, hid = w_rel.shape
    fcols = two_f // 2
    feats, rows = x_rows.shape

    def kernel(at, w_ref, x_ref, b_ref, pre_ref, wn_ref, ws):
        for j in range(ny):
            for k in range(nv):
                z = lax.rem(at[1] + lax.bitwise_xor(at[0], k), nv)
                y = lax.bitwise_xor(at[2], j)
                start = pl.multiple_of((z * ny + y) * fcols, fcols)
                ws[pl.ds(start, fcols), :] = w_ref[j, k, :fcols, :]
                wn_ref[pl.ds(start, fcols), :] = w_ref[j, k, fcols:, :]
        pre_ref[...] = contract_rows(x_ref[...], ws[...]) + b_ref[...]

    return pl.pallas_call(
        kernel,
        in_specs=[pl.BlockSpec(memory_space=pltpu.SMEM)]
        + [pl.BlockSpec(memory_space=pltpu.VMEM)] * 3,
        out_specs=[pl.BlockSpec(memory_space=pltpu.VMEM)] * 2,
        out_shape=[
            jax.ShapeDtypeStruct((rows, hid), F32),
            jax.ShapeDtypeStruct((feats, hid), BF16),
        ],
        scratch_shapes=[pltpu.VMEM((feats, hid), BF16)],
        name="own_part",
        compiler_params=pltpu.CompilerParams(vmem_limit_bytes=40 << 20),
        cost_estimate=pl.CostEstimate(
            flops=2 * feats * rows * hid, bytes_accessed=4 << 20, transcendentals=0
        ),
    )(place, w_rel, x_rows, bias)


def layer(place, pre_own, a_rows, w_neigh, x_rows, upstream):
    feats, rows = x_rows.shape
    hid = upstream.shape[1]

    def kernel(at, pre_ref, a_ref, wn_ref, x_ref, up_ref, hid_ref, g_ref, gb_ref):
        v = pre_ref[...] + contract_rows(a_ref[...], wn_ref[...])
        sq = v * v
        t = jnp.tanh(GELU_A * (v + GELU_B * sq * v))
        half = 0.5 * (1.0 + t)
        hid_ref[...] = (v * half).astype(BF16)
        slope = half + 0.5 * v * (1.0 - t * t) * (GELU_A * (1.0 + 3.0 * GELU_B * sq))
        delta = (up_ref[...].astype(F32) * slope).astype(BF16)
        gb_ref[...] = jnp.sum(delta.astype(F32), axis=0, keepdims=True)
        core = lax.rem(at[0], 2)
        g_ref[core] = jnp.dot(x_ref[...], delta, preferred_element_type=F32).astype(BF16)
        g_ref[1 - core] = jnp.dot(a_ref[...], delta, preferred_element_type=F32).astype(BF16)

    return pl.pallas_call(
        kernel,
        in_specs=[pl.BlockSpec(memory_space=pltpu.SMEM)]
        + [pl.BlockSpec(memory_space=pltpu.VMEM)] * 5,
        out_specs=[pl.BlockSpec(memory_space=pltpu.VMEM)] * 3,
        out_shape=[
            jax.ShapeDtypeStruct((rows, hid), BF16),
            jax.ShapeDtypeStruct((2, feats, hid), BF16),
            jax.ShapeDtypeStruct((1, hid), F32),
        ],
        name="layer",
        compiler_params=pltpu.CompilerParams(vmem_limit_bytes=40 << 20),
        cost_estimate=pl.CostEstimate(
            flops=6 * feats * rows * hid, bytes_accessed=6 << 20, transcendentals=rows * hid
        ),
    )(place, pre_own, a_rows, w_neigh, x_rows, upstream)


def body(nz, ny, features_t, tile_weights, tile_dst, tile_src, tile_count, w_self, w_neigh, bias, grad_hidden):
    feats = features_t[0]
    fcols, nsrc = feats.shape
    nv = lax.axis_size("vgroup")
    nfeat = lax.axis_size("feat")
    rows_dev, hid = grad_hidden.shape
    ndst = rows_dev * nfeat
    v = lax.axis_index("vgroup")
    f = lax.axis_index("feat")
    place = jnp.stack([v, f // ny, f % ny]).astype(jnp.int32)

    with jax.named_scope("send_features"):
        x_out = feats[:, :ndst].reshape(fcols, nfeat, rows_dev).transpose(1, 0, 2)
        x_rows = lax.all_to_all(x_out, "feat", 0, 0, tiled=True).reshape(nfeat * fcols, rows_dev)

    with jax.named_scope("gather_weights"):
        own = jnp.concatenate([w_self, w_neigh], axis=0)
        shift = [
            (a * nfeat + z * ny + y, a * nfeat + ((z - a) % nz) * ny + y)
            for a in range(nv)
            for z in range(nz)
            for y in range(ny)
        ]
        one = lax.ppermute(own, ("vgroup", "feat"), shift)
        column = jnp.stack(
            [one]
            + [lax.ppermute(one, "vgroup", [(a, a ^ k) for a in range(nv)]) for k in range(1, nv)]
        )
        w_rel = jnp.stack(
            [column]
            + [
                lax.ppermute(column, "feat", [(a, (a // ny) * ny + ((a % ny) ^ j)) for a in range(nfeat)])
                for j in range(1, ny)
            ]
        )

    agg = aggregate(tile_dst[0], tile_src[0], tile_count, feats, tile_weights[0], nfeat)
    with jax.named_scope("send_aggregated"):
        a_rows = lax.all_to_all(agg, "feat", 0, 0, tiled=True).reshape(nfeat * fcols, rows_dev)

    pre_own, wn = own_part(place, w_rel, x_rows, bias[None, :])
    hidden, grads, gb = layer(place, pre_own, a_rows, wn, x_rows, grad_hidden)

    with jax.named_scope("reduce_grads"):
        other_core = [(a, a ^ 1) for a in range(nv)]
        got = lax.ppermute(grads[1], "vgroup", other_core)
        pair = (grads[0].astype(F32) + got.astype(F32)).astype(BF16).reshape(nfeat, fcols, hid)
        gb = gb + lax.ppermute(gb, "vgroup", other_core)
        high = lax.reduce_precision(gb, 8, 7)
        mid = lax.reduce_precision(gb - high, 8, 7)
        low = gb - high - mid
        split = jnp.concatenate([high, mid, low, jnp.zeros((5, hid), F32)], 0).astype(BF16)
        outgoing = jnp.concatenate([pair, jnp.broadcast_to(split[None], (nfeat, 8, hid))], axis=1)
        arrived = lax.all_to_all(outgoing, "feat", 0, 0, tiled=True)
        total = jnp.sum(arrived.astype(F32), axis=0)
        parts = [total] + [
            lax.ppermute(total, "vgroup", [(a, a ^ (2 * k)) for a in range(nv)]) for k in range(1, nv // 2)
        ]
        total = sum(parts[1:], parts[0])
        other = lax.ppermute(total[:fcols], "vgroup", other_core)
        first = v % 2 == 0
        mine = total[:fcols]
        grad_self = jnp.where(first, mine, other)
        grad_neigh = jnp.where(first, other, mine)
        grad_bias = jnp.sum(total[fcols:], axis=0)
    return (hidden, grad_self, grad_neigh, grad_bias)


def solution(mesh):
    ny = 4
    nz = mesh.shape["feat"] // ny

    def run(*args):
        return body(nz, ny, *args)

    return jax.shard_map(
        run,
        mesh=mesh,
        in_specs=(
            P("vgroup", "feat", None),
            P("vgroup", None, None, None),
            P("vgroup", None),
            P("vgroup", None),
            P("vgroup"),
            P("feat", None),
            P("feat", None),
            P(),
            P(("vgroup", "feat"), None),
        ),
        out_specs=(P(("vgroup", "feat"), None), P("feat", None), P("feat", None), P()),
        check_vma=False,
    )
```

```python
import jax
import jax.numpy as jnp
from jax import lax
from jax.experimental import pallas as pl
from jax.experimental.pallas import tpu as pltpu
from jax.sharding import PartitionSpec as P

TILE = 128
SLOTS_STEP = 128
UNROLL = 32
GELU_A = 0.7978845608
GELU_B = 0.044715
BF16 = jnp.bfloat16
F32 = jnp.float32


def aggregate(dsts, srcs, count, feats, weights, nfeat):
    fcols, nsrc = feats.shape
    slots = weights.shape[0]
    dtiles = nsrc // TILE // 2
    per_owner = dtiles // nfeat
    steps = slots // SLOTS_STEP

    def kernel(dst, src, cnt, x_ref, w_ref, o_ref, acc, out, sem):
        i = pl.program_id(0)

        @pl.when(i == 0)
        def _():
            acc[...] = jnp.zeros_like(acc)

        base = i * SLOTS_STEP
        live = jnp.clip(cnt[0] - base, 0, SLOTS_STEP)
        zero = jnp.zeros((fcols, TILE), BF16)

        def source(slot):
            return x_ref[:, pl.ds(pl.multiple_of(src[slot] * TILE, TILE), TILE)]

        def group(g, carry):
            first = g * UNROLL
            products = []
            for u in range(0, UNROLL, 2):
                slot = base + first + u
                left = jnp.concatenate(
                    [
                        jnp.concatenate([source(slot), zero], 1),
                        jnp.concatenate([zero, source(slot + 1)], 1),
                    ],
                    0,
                )
                right = jnp.concatenate([w_ref[first + u], w_ref[first + u + 1]], 1)
                both = lax.dot_general(
                    left, right, (((1,), (1,)), ((), ())), preferred_element_type=F32
                )
                products += [both[:fcols], both[fcols:]]
            for u in range(UNROLL):
                slot = base + first + u
                acc[dst[slot]] += jnp.where(slot < cnt[0], products[u], 0.0)
            return carry

        lax.fori_loop(0, pl.cdiv(live, UNROLL), group, 0)

        @pl.when(i == steps - 1)
        def _():
            part = nfeat // 4
            copies = []
            for p in range(4):
                tiles = acc[p * part * per_owner : (p + 1) * part * per_owner]
                out[p * part : (p + 1) * part] = tiles.reshape(part, per_owner * fcols, TILE).astype(BF16)
                copies.append(
                    pltpu.make_async_copy(
                        out.at[pl.ds(p * part, part)], o_ref.at[pl.ds(p * part, part)], sem.at[p]
                    )
                )
                copies[-1].start()
            for c in copies:
                c.wait()

    return pl.pallas_call(
        kernel,
        grid_spec=pltpu.PrefetchScalarGridSpec(
            num_scalar_prefetch=3,
            grid=(steps,),
            in_specs=[
                pl.BlockSpec((fcols, nsrc), lambda i, *_: (0, 0)),
                pl.BlockSpec((SLOTS_STEP, TILE, TILE), lambda i, *_: (i, 0, 0)),
            ],
            out_specs=pl.BlockSpec(memory_space=pltpu.HBM),
            scratch_shapes=[
                pltpu.VMEM((dtiles, fcols, TILE), F32),
                pltpu.VMEM((nfeat, per_owner * fcols, TILE), BF16),
                pltpu.SemaphoreType.DMA((4,)),
            ],
        ),
        out_shape=jax.ShapeDtypeStruct((nfeat, per_owner * fcols, TILE), BF16),
        name="aggregate",
        compiler_params=pltpu.CompilerParams(vmem_limit_bytes=40 << 20),
        cost_estimate=pl.CostEstimate(
            flops=2 * slots * fcols * TILE * TILE,
            bytes_accessed=slots * TILE * TILE * 2 + fcols * nsrc * 2,
            transcendentals=0,
        ),
    )(dsts, srcs, count, feats, weights)


def contract_rows(a, b):
    return lax.dot_general(a, b, (((0,), (0,)), ((), ())), preferred_element_type=F32)


def in_vmem(n):
    return [pl.BlockSpec(memory_space=pltpu.VMEM)] * n


def pack(place, feats, w_self, w_neigh, nfeat, rows_dev):
    fcols = feats.shape[0]
    hid = w_self.shape[1]
    per_owner = rows_dev // TILE
    share = fcols // 2

    def kernel(at, x_ref, ws_ref, wn_ref, o_ref, both):
        both[:, :hid] = ws_ref[...]
        both[:, hid:] = wn_ref[...]
        core, x = lax.rem(at[0], 2), lax.div(at[0], 2)
        piece = both[pl.ds(pl.multiple_of(core * share, share), share), pl.ds(pl.multiple_of(x * TILE, TILE), TILE)]
        for c in range(nfeat):
            for q in range(per_owner):
                tile = c * per_owner + q
                o_ref[c, q * fcols : (q + 1) * fcols, :] = x_ref[:, tile * TILE : (tile + 1) * TILE]
            o_ref[c, per_owner * fcols :, :] = piece

    return pl.pallas_call(
        kernel,
        grid=(1,),
        in_specs=[
            pl.BlockSpec(memory_space=pltpu.SMEM),
            pl.BlockSpec((fcols, nfeat * rows_dev), lambda i: (0, 0)),
            pl.BlockSpec((fcols, hid), lambda i: (0, 0)),
            pl.BlockSpec((fcols, hid), lambda i: (0, 0)),
        ],
        out_specs=pl.BlockSpec((nfeat, per_owner * fcols + share, TILE), lambda i: (0, 0, 0)),
        out_shape=jax.ShapeDtypeStruct((nfeat, per_owner * fcols + share, TILE), BF16),
        scratch_shapes=[pltpu.VMEM((fcols, 2 * hid), BF16)],
        name="pack",
        compiler_params=pltpu.CompilerParams(vmem_limit_bytes=16 << 20),
        cost_estimate=pl.CostEstimate(flops=0, bytes_accessed=3 << 20, transcendentals=0),
    )(place, feats, w_self, w_neigh)


def contract_rows(a, b):
    return lax.dot_general(a, b, (((0,), (0,)), ((), ())), preferred_element_type=F32)


def row_tile(ref, q, fcols):
    return ref[:, q * fcols : (q + 1) * fcols, :].reshape(ref.shape[0] * fcols, TILE)


def own_part(place, same_core, other_core, x_rows, bias, tiles):
    nx, nfeat, share, _ = same_core.shape
    hid = bias.shape[1]
    fcols = 2 * share

    def kernel(at, w0, w1, x_ref, b_ref, pre_ref, wn_ref, both):
        for k in range(nx):
            x = lax.bitwise_xor(lax.div(at[0], 2), k)
            lanes = pl.ds(pl.multiple_of(x * TILE, TILE), TILE)
            for r, ref in enumerate((w0, w1)):
                core = lax.bitwise_xor(lax.rem(at[0], 2), r)
                both[:, pl.ds(pl.multiple_of(core * share, share), share), lanes] = ref[k]
        ws = both[:, :, :hid].reshape(nfeat * fcols, hid)
        wn_ref[...] = both[:, :, hid:].reshape(nfeat * fcols, hid)
        for q in range(tiles):
            pre_ref[q] = contract_rows(row_tile(x_ref, q, fcols), ws) + b_ref[...]

    return pl.pallas_call(
        kernel,
        in_specs=[pl.BlockSpec(memory_space=pltpu.SMEM)] + in_vmem(4),
        out_specs=in_vmem(2),
        out_shape=[
            jax.ShapeDtypeStruct((tiles, TILE, hid), F32),
            jax.ShapeDtypeStruct((nfeat * fcols, hid), BF16),
        ],
        scratch_shapes=[pltpu.VMEM((nfeat, fcols, 2 * hid), BF16)],
        name="own_part",
        compiler_params=pltpu.CompilerParams(vmem_limit_bytes=16 << 20),
        cost_estimate=pl.CostEstimate(
            flops=2 * nfeat * fcols * tiles * TILE * hid, bytes_accessed=4 << 20, transcendentals=0
        ),
    )(place, same_core, other_core, x_rows, bias)


def layer(place, pre_own, a_rows, w_neigh, x_rows, upstream):
    nfeat = x_rows.shape[0]
    feats, hid = w_neigh.shape
    fcols = feats // nfeat
    rows = upstream.shape[0]
    tiles = rows // TILE
    halves = hid // TILE
    out_rows = halves * fcols + 8

    def kernel(at, pre_hbm, a_ref, wn_hbm, x_ref, up_ref, hid_ref, g_ref, pre, wn, deltas, sem):
        get_wn = pltpu.make_async_copy(wn_hbm, wn, sem.at[0])
        get_pre = pltpu.make_async_copy(pre_hbm, pre, sem.at[1])
        get_wn.start()
        get_pre.start()
        get_wn.wait()
        get_pre.wait()
        gb = jnp.zeros((1, hid), F32)
        for q in range(tiles):
            here = slice(q * TILE, (q + 1) * TILE)
            v = pre[q] + contract_rows(row_tile(a_ref, q, fcols), wn[...])
            sq = v * v
            t = jnp.tanh(GELU_A * (v + GELU_B * sq * v))
            half = 0.5 * (1.0 + t)
            hid_ref[here, :] = (v * half).astype(BF16)
            slope = half + 0.5 * v * (1.0 - t * t) * (GELU_A * (1.0 + 3.0 * GELU_B * sq))
            delta = (up_ref[here, :].astype(F32) * slope).astype(BF16)
            deltas[here, :] = delta
            gb = gb + jnp.sum(delta.astype(F32), axis=0, keepdims=True)
        core = lax.rem(at[0], 2)
        for slot, ref in ((core, x_ref), (1 - core, a_ref)):
            left = jnp.concatenate([row_tile(ref, q, fcols) for q in range(tiles)], axis=1)
            grad = jnp.dot(left, deltas[...], preferred_element_type=F32).astype(BF16)
            for h in range(halves):
                g_ref[slot, :, h * fcols : (h + 1) * fcols, :] = grad[:, h * TILE : (h + 1) * TILE].reshape(
                    nfeat, fcols, TILE
                )
        high = gb.astype(BF16).astype(F32)
        mid = (gb - high).astype(BF16).astype(F32)
        low = gb - high - mid
        lines = [part[:, h * TILE : (h + 1) * TILE] for part in (high, mid, low) for h in range(halves)]
        lines = jnp.concatenate(lines + [jnp.zeros((8 - len(lines), TILE), F32)], axis=0).astype(BF16)
        g_ref[0, :, halves * fcols :, :] = jnp.broadcast_to(lines[None], (nfeat, 8, TILE))
        g_ref[1, :, halves * fcols :, :] = jnp.zeros((nfeat, 8, TILE), BF16)

    return pl.pallas_call(
        kernel,
        in_specs=[
            pl.BlockSpec(memory_space=pltpu.SMEM),
            pl.BlockSpec(memory_space=pl.ANY),
            *in_vmem(1),
            pl.BlockSpec(memory_space=pl.ANY),
            *in_vmem(2),
        ],
        out_specs=in_vmem(2),
        out_shape=[
            jax.ShapeDtypeStruct((rows, hid), BF16),
            jax.ShapeDtypeStruct((2, nfeat, out_rows, TILE), BF16),
        ],
        scratch_shapes=[
            pltpu.VMEM((tiles, TILE, hid), F32),
            pltpu.VMEM((feats, hid), BF16),
            pltpu.VMEM((rows, hid), BF16),
            pltpu.SemaphoreType.DMA((2,)),
        ],
        name="layer",
        compiler_params=pltpu.CompilerParams(vmem_limit_bytes=24 << 20),
        cost_estimate=pl.CostEstimate(
            flops=6 * feats * rows * hid, bytes_accessed=6 << 20, transcendentals=rows * hid
        ),
    )(place, pre_own, a_rows, w_neigh, x_rows, upstream)


def finish(place, terms, fcols, hid):
    halves = hid // TILE

    def kernel(at, *refs):
        ins, (gs_ref, gn_ref, gb_ref) = refs[: len(terms)], refs[len(terms) :]
        mine = sum(ref[...] for ref in ins[0::2])
        other = sum(ref[...] for ref in ins[1::2])
        first = lax.rem(at[0], 2) == 0
        both = mine + other
        for h in range(halves):
            lanes, rows = slice(h * TILE, (h + 1) * TILE), slice(h * fcols, (h + 1) * fcols)
            gs_ref[:, lanes] = jnp.where(first, mine[rows], other[rows])
            gn_ref[:, lanes] = jnp.where(first, other[rows], mine[rows])
            at_row = halves * fcols + h
            gb_ref[:, lanes] = sum(both[at_row + halves * p : at_row + halves * p + 1] for p in range(3))

    return pl.pallas_call(
        kernel,
        in_specs=[pl.BlockSpec(memory_space=pltpu.SMEM)] + in_vmem(len(terms)),
        out_specs=in_vmem(3),
        out_shape=[
            jax.ShapeDtypeStruct((fcols, hid), F32),
            jax.ShapeDtypeStruct((fcols, hid), F32),
            jax.ShapeDtypeStruct((1, hid), F32),
        ],
        name="finish",
        compiler_params=pltpu.CompilerParams(vmem_limit_bytes=8 << 20),
    )(place, *terms)


def body(features_t, tile_weights, tile_dst, tile_src, tile_count, w_self, w_neigh, bias, grad_hidden):
    feats = features_t[0]
    fcols = feats.shape[0]
    nv = lax.axis_size("vgroup")
    nfeat = lax.axis_size("feat")
    rows_dev, hid = grad_hidden.shape
    tiles = rows_dev // TILE
    place = lax.axis_index("vgroup")[None].astype(jnp.int32)

    def direct(value, bits):
        return [lax.ppermute(value, "vgroup", [(a, a ^ bit) for a in range(nv)]) for bit in bits]

    with jax.named_scope("send_features"):
        outgoing = pack(place, feats, w_self, w_neigh, nfeat, rows_dev)
        x_rows = lax.all_to_all(outgoing, "feat", 0, 0, tiled=True)

    agg = aggregate(tile_dst[0], tile_src[0], tile_count, feats, tile_weights[0], nfeat)
    x_rows, agg = lax.optimization_barrier((x_rows, agg))
    with jax.named_scope("send_aggregated"):
        a_rows = lax.all_to_all(agg, "feat", 0, 0, tiled=True)

    with jax.named_scope("weights_over_vgroup"):
        piece = x_rows[:, tiles * fcols :, :]
        same_core = jnp.stack([piece] + direct(piece, (2, 4, 6)))
        [other_core] = direct(same_core, (1,))

    pre_own, wn = own_part(place, same_core, other_core, x_rows, bias[None, :], tiles)
    hidden, grads = layer(place, pre_own, a_rows, wn, x_rows, grad_hidden)

    with jax.named_scope("reduce_grads"):
        [got] = direct(grads[1], (1,))
        pair = (grads[0].astype(F32) + got.astype(F32)).astype(BF16)
        arrived = lax.all_to_all(pair, "feat", 0, 0, tiled=True)
        total = jnp.sum(arrived.astype(F32), axis=0)
        terms = [total] + direct(total, range(1, nv))
        grad_self, grad_neigh, grad_bias = finish(place, terms, fcols, hid)
    return (hidden, grad_self, grad_neigh, grad_bias[0])


def solution(mesh):
    return jax.shard_map(
        body,
        mesh=mesh,
        in_specs=(
            P("vgroup", "feat", None),
            P("vgroup", None, None, None),
            P("vgroup", None),
            P("vgroup", None),
            P("vgroup"),
            P("feat", None),
            P("feat", None),
            P(),
            P(("vgroup", "feat"), None),
        ),
        out_specs=(P(("vgroup", "feat"), None), P("feat", None), P("feat", None), P()),
        check_vma=False,
    )
```

```python
import jax
import jax.numpy as jnp
from jax import lax
from jax.experimental import pallas as pl
from jax.experimental.pallas import tpu as pltpu
from jax.sharding import PartitionSpec as P

TILE = 128
SLOTS_STEP = 128
UNROLL = 32
GELU_A = 0.7978845608
GELU_B = 0.044715
BF16 = jnp.bfloat16
F32 = jnp.float32


def aggregate(dsts, srcs, count, feats, weights, nfeat):
    fcols, nsrc = feats.shape
    slots = weights.shape[0]
    dtiles = nsrc // TILE // 2
    per_owner = dtiles // nfeat
    steps = slots // SLOTS_STEP

    def kernel(dst, src, cnt, x_ref, w_ref, o_ref, acc, out, sem):
        i = pl.program_id(0)

        @pl.when(i == 0)
        def _():
            acc[...] = jnp.zeros_like(acc)

        base = i * SLOTS_STEP
        live = jnp.clip(cnt[0] - base, 0, SLOTS_STEP)
        zero = jnp.zeros((fcols, TILE), BF16)

        def source(slot):
            return x_ref[:, pl.ds(pl.multiple_of(src[slot] * TILE, TILE), TILE)]

        def group(g, carry):
            first = g * UNROLL
            products = []
            for u in range(0, UNROLL, 2):
                slot = base + first + u
                left = jnp.concatenate(
                    [
                        jnp.concatenate([source(slot), zero], 1),
                        jnp.concatenate([zero, source(slot + 1)], 1),
                    ],
                    0,
                )
                right = jnp.concatenate([w_ref[first + u], w_ref[first + u + 1]], 1)
                both = lax.dot_general(
                    left, right, (((1,), (1,)), ((), ())), preferred_element_type=F32
                )
                products += [both[:fcols], both[fcols:]]
            for u in range(UNROLL):
                slot = base + first + u
                acc[dst[slot]] += jnp.where(slot < cnt[0], products[u], 0.0)
            return carry

        lax.fori_loop(0, pl.cdiv(live, UNROLL), group, 0)

        @pl.when(i == steps - 1)
        def _():
            part = nfeat // 4
            copies = []
            for p in range(4):
                tiles = acc[p * part * per_owner : (p + 1) * part * per_owner]
                out[p * part : (p + 1) * part] = tiles.reshape(part, per_owner * fcols, TILE).astype(BF16)
                copies.append(
                    pltpu.make_async_copy(
                        out.at[pl.ds(p * part, part)], o_ref.at[pl.ds(p * part, part)], sem.at[p]
                    )
                )
                copies[-1].start()
            for c in copies:
                c.wait()

    return pl.pallas_call(
        kernel,
        grid_spec=pltpu.PrefetchScalarGridSpec(
            num_scalar_prefetch=3,
            grid=(steps,),
            in_specs=[
                pl.BlockSpec((fcols, nsrc), lambda i, *_: (0, 0)),
                pl.BlockSpec((SLOTS_STEP, TILE, TILE), lambda i, *_: (i, 0, 0)),
            ],
            out_specs=pl.BlockSpec(memory_space=pltpu.HBM),
            scratch_shapes=[
                pltpu.VMEM((dtiles, fcols, TILE), F32),
                pltpu.VMEM((nfeat, per_owner * fcols, TILE), BF16),
                pltpu.SemaphoreType.DMA((4,)),
            ],
        ),
        out_shape=jax.ShapeDtypeStruct((nfeat, per_owner * fcols, TILE), BF16),
        name="aggregate",
        compiler_params=pltpu.CompilerParams(vmem_limit_bytes=40 << 20),
        cost_estimate=pl.CostEstimate(
            flops=2 * slots * fcols * TILE * TILE,
            bytes_accessed=slots * TILE * TILE * 2 + fcols * nsrc * 2,
            transcendentals=0,
        ),
    )(dsts, srcs, count, feats, weights)


def contract_rows(a, b):
    return lax.dot_general(a, b, (((0,), (0,)), ((), ())), preferred_element_type=F32)


def in_vmem(n):
    return [pl.BlockSpec(memory_space=pltpu.VMEM)] * n


def pack(place, feats, w_self, w_neigh, nfeat, rows_dev):
    fcols = feats.shape[0]
    hid = w_self.shape[1]
    per_owner = rows_dev // TILE
    share = fcols // 2

    parts = 4
    owners = nfeat // parts

    def kernel(at, x_hbm, ws_hbm, wn_hbm, o_hbm, x_ref, o_ref, both, sem_x, sem_o, sem_w):
        get_w = [
            pltpu.make_async_copy(ws_hbm, both.at[:, pl.ds(0, hid)], sem_w.at[0]),
            pltpu.make_async_copy(wn_hbm, both.at[:, pl.ds(hid, hid)], sem_w.at[1]),
        ]
        width = owners * rows_dev
        get_x = [
            pltpu.make_async_copy(
                x_hbm.at[:, pl.ds(p * width, width)], x_ref.at[:, pl.ds(p * width, width)], sem_x.at[p]
            )
            for p in range(parts)
        ]
        put = [
            pltpu.make_async_copy(
                o_ref.at[pl.ds(p * owners, owners)], o_hbm.at[pl.ds(p * owners, owners)], sem_o.at[p]
            )
            for p in range(parts)
        ]
        for c in get_w + get_x:
            c.start()
        for c in get_w:
            c.wait()
        core, x = lax.rem(at[0], 2), lax.div(at[0], 2)
        piece = both[pl.ds(pl.multiple_of(core * share, share), share), pl.ds(pl.multiple_of(x * TILE, TILE), TILE)]
        for p in range(parts):
            get_x[p].wait()
            for c in range(p * owners, (p + 1) * owners):
                for q in range(per_owner):
                    tile = c * per_owner + q
                    o_ref[c, q * fcols : (q + 1) * fcols, :] = x_ref[:, tile * TILE : (tile + 1) * TILE]
                o_ref[c, per_owner * fcols :, :] = piece
            put[p].start()
        for c in put:
            c.wait()

    out = (nfeat, per_owner * fcols + share, TILE)
    return pl.pallas_call(
        kernel,
        in_specs=[pl.BlockSpec(memory_space=pltpu.SMEM)] + [pl.BlockSpec(memory_space=pl.ANY)] * 3,
        out_specs=pl.BlockSpec(memory_space=pl.ANY),
        out_shape=jax.ShapeDtypeStruct(out, BF16),
        scratch_shapes=[
            pltpu.VMEM((fcols, nfeat * rows_dev), BF16),
            pltpu.VMEM(out, BF16),
            pltpu.VMEM((fcols, 2 * hid), BF16),
            pltpu.SemaphoreType.DMA((parts,)),
            pltpu.SemaphoreType.DMA((parts,)),
            pltpu.SemaphoreType.DMA((2,)),
        ],
        name="pack",
        compiler_params=pltpu.CompilerParams(vmem_limit_bytes=60 << 20),
        cost_estimate=pl.CostEstimate(flops=0, bytes_accessed=3 << 20, transcendentals=0),
    )(place, feats, w_self, w_neigh)


def contract_rows(a, b):
    return lax.dot_general(a, b, (((0,), (0,)), ((), ())), preferred_element_type=F32)


def row_tile(ref, q, fcols):
    return ref[:, q * fcols : (q + 1) * fcols, :].reshape(ref.shape[0] * fcols, TILE)


def own_part(place, same_core, other_core, x_rows, bias, tiles):
    nx, nfeat, share, _ = same_core.shape
    hid = bias.shape[1]
    fcols = 2 * share

    def kernel(at, w0, w1, x_ref, b_ref, pre_ref, wn_ref, both):
        for k in range(nx):
            x = lax.bitwise_xor(lax.div(at[0], 2), k)
            lanes = pl.ds(pl.multiple_of(x * TILE, TILE), TILE)
            for r, ref in enumerate((w0, w1)):
                core = lax.bitwise_xor(lax.rem(at[0], 2), r)
                both[:, pl.ds(pl.multiple_of(core * share, share), share), lanes] = ref[k]
        ws = both[:, :, :hid].reshape(nfeat * fcols, hid)
        wn_ref[...] = both[:, :, hid:].reshape(nfeat * fcols, hid)
        for q in range(tiles):
            pre_ref[q] = contract_rows(row_tile(x_ref, q, fcols), ws) + b_ref[...]

    return pl.pallas_call(
        kernel,
        in_specs=[pl.BlockSpec(memory_space=pltpu.SMEM)] + in_vmem(4),
        out_specs=in_vmem(2),
        out_shape=[
            jax.ShapeDtypeStruct((tiles, TILE, hid), F32),
            jax.ShapeDtypeStruct((nfeat * fcols, hid), BF16),
        ],
        scratch_shapes=[pltpu.VMEM((nfeat, fcols, 2 * hid), BF16)],
        name="own_part",
        compiler_params=pltpu.CompilerParams(vmem_limit_bytes=16 << 20),
        cost_estimate=pl.CostEstimate(
            flops=2 * nfeat * fcols * tiles * TILE * hid, bytes_accessed=4 << 20, transcendentals=0
        ),
    )(place, same_core, other_core, x_rows, bias)


def layer(place, pre_own, a_rows, w_neigh, x_rows, upstream):
    nfeat = x_rows.shape[0]
    feats, hid = w_neigh.shape
    fcols = feats // nfeat
    rows = upstream.shape[0]
    tiles = rows // TILE
    halves = hid // TILE
    out_rows = halves * fcols + 8

    def kernel(at, pre, a_ref, wn, x_ref, up_ref, hid_ref, g_ref, deltas):
        gb = jnp.zeros((1, hid), F32)
        for q in range(tiles):
            here = slice(q * TILE, (q + 1) * TILE)
            v = pre[q] + contract_rows(row_tile(a_ref, q, fcols), wn[...])
            sq = v * v
            t = jnp.tanh(GELU_A * (v + GELU_B * sq * v))
            half = 0.5 * (1.0 + t)
            hid_ref[here, :] = (v * half).astype(BF16)
            slope = half + 0.5 * v * (1.0 - t * t) * (GELU_A * (1.0 + 3.0 * GELU_B * sq))
            delta = (up_ref[here, :].astype(F32) * slope).astype(BF16)
            deltas[here, :] = delta
            gb = gb + jnp.sum(delta.astype(F32), axis=0, keepdims=True)
        core = lax.rem(at[0], 2)
        for slot, ref in ((core, x_ref), (1 - core, a_ref)):
            left = jnp.concatenate([row_tile(ref, q, fcols) for q in range(tiles)], axis=1)
            grad = jnp.dot(left, deltas[...], preferred_element_type=F32).astype(BF16)
            for h in range(halves):
                g_ref[slot, :, h * fcols : (h + 1) * fcols, :] = grad[:, h * TILE : (h + 1) * TILE].reshape(
                    nfeat, fcols, TILE
                )
        high = gb.astype(BF16).astype(F32)
        mid = (gb - high).astype(BF16).astype(F32)
        low = gb - high - mid
        lines = [part[:, h * TILE : (h + 1) * TILE] for part in (high, mid, low) for h in range(halves)]
        lines = jnp.concatenate(lines + [jnp.zeros((8 - len(lines), TILE), F32)], axis=0).astype(BF16)
        g_ref[0, :, halves * fcols :, :] = jnp.broadcast_to(lines[None], (nfeat, 8, TILE))
        g_ref[1, :, halves * fcols :, :] = jnp.zeros((nfeat, 8, TILE), BF16)

    return pl.pallas_call(
        kernel,
        in_specs=[pl.BlockSpec(memory_space=pltpu.SMEM)] + in_vmem(5),
        out_specs=in_vmem(2),
        out_shape=[
            jax.ShapeDtypeStruct((rows, hid), BF16),
            jax.ShapeDtypeStruct((2, nfeat, out_rows, TILE), BF16),
        ],
        scratch_shapes=[pltpu.VMEM((rows, hid), BF16)],
        name="layer",
        compiler_params=pltpu.CompilerParams(vmem_limit_bytes=24 << 20),
        cost_estimate=pl.CostEstimate(
            flops=6 * feats * rows * hid, bytes_accessed=6 << 20, transcendentals=rows * hid
        ),
    )(place, pre_own, a_rows, w_neigh, x_rows, upstream)


def finish(place, mine, other, fcols):
    halves = (mine.shape[0] - 8) // fcols
    hid = halves * TILE

    def kernel(at, m_ref, o_ref, gs_ref, gn_ref, gb_ref):
        first = lax.rem(at[0], 2) == 0
        for h in range(halves):
            lanes, rows = slice(h * TILE, (h + 1) * TILE), slice(h * fcols, (h + 1) * fcols)
            gs_ref[:, lanes] = jnp.where(first, m_ref[rows], o_ref[rows])
            gn_ref[:, lanes] = jnp.where(first, o_ref[rows], m_ref[rows])
        both = m_ref[halves * fcols :] + o_ref[halves * fcols :]
        for h in range(halves):
            parts = [both[halves * p + h : halves * p + h + 1] for p in range(3)]
            gb_ref[:, h * TILE : (h + 1) * TILE] = parts[0] + parts[1] + parts[2]

    return pl.pallas_call(
        kernel,
        in_specs=[pl.BlockSpec(memory_space=pltpu.SMEM)] + in_vmem(2),
        out_specs=in_vmem(3),
        out_shape=[
            jax.ShapeDtypeStruct((fcols, hid), F32),
            jax.ShapeDtypeStruct((fcols, hid), F32),
            jax.ShapeDtypeStruct((1, hid), F32),
        ],
        name="finish",
        compiler_params=pltpu.CompilerParams(vmem_limit_bytes=8 << 20),
    )(place, mine, other)


def body(features_t, tile_weights, tile_dst, tile_src, tile_count, w_self, w_neigh, bias, grad_hidden):
    feats = features_t[0]
    fcols = feats.shape[0]
    nv = lax.axis_size("vgroup")
    nfeat = lax.axis_size("feat")
    rows_dev, hid = grad_hidden.shape
    tiles = rows_dev // TILE
    place = lax.axis_index("vgroup")[None].astype(jnp.int32)

    def direct(value, bits):
        return [lax.ppermute(value, "vgroup", [(a, a ^ bit) for a in range(nv)]) for bit in bits]

    with jax.named_scope("send_features"):
        outgoing = pack(place, feats, w_self, w_neigh, nfeat, rows_dev)
        x_rows = lax.all_to_all(outgoing, "feat", 0, 0, tiled=True)

    agg = aggregate(tile_dst[0], tile_src[0], tile_count, feats, tile_weights[0], nfeat)
    x_rows, agg = lax.optimization_barrier((x_rows, agg))
    with jax.named_scope("send_aggregated"):
        a_rows = lax.all_to_all(agg, "feat", 0, 0, tiled=True)

    with jax.named_scope("weights_over_vgroup"):
        piece = x_rows[:, tiles * fcols :, :]
        same_core = jnp.stack([piece] + direct(piece, (2, 4, 6)))
        [other_core] = direct(same_core, (1,))

    pre_own, wn = own_part(place, same_core, other_core, x_rows, bias[None, :], tiles)
    hidden, grads = layer(place, pre_own, a_rows, wn, x_rows, grad_hidden)

    with jax.named_scope("reduce_grads"):
        [got] = direct(grads[1], (1,))
        pair = (grads[0].astype(F32) + got.astype(F32)).astype(BF16)
        arrived = lax.all_to_all(pair, "feat", 0, 0, tiled=True)
        total = jnp.sum(arrived.astype(F32), axis=0)
        total = sum(direct(total, (2, 4, 6)), total)
        [other] = direct(total, (1,))
        grad_self, grad_neigh, grad_bias = finish(place, total, other, fcols)
    return (hidden, grad_self, grad_neigh, grad_bias[0])


def solution(mesh):
    return jax.shard_map(
        body,
        mesh=mesh,
        in_specs=(
            P("vgroup", "feat", None),
            P("vgroup", None, None, None),
            P("vgroup", None),
            P("vgroup", None),
            P("vgroup"),
            P("feat", None),
            P("feat", None),
            P(),
            P(("vgroup", "feat"), None),
        ),
        out_specs=(P(("vgroup", "feat"), None), P("feat", None), P("feat", None), P()),
        check_vma=False,
    )
```

```python
import jax
import jax.numpy as jnp
from jax import lax
from jax.experimental import pallas as pl
from jax.experimental.pallas import tpu as pltpu
from jax.sharding import PartitionSpec as P

TILE = 128
SLOTS_STEP = 64
BUFFERS = 4
GELU_A = 0.7978845608
GELU_B = 0.044715
BF16 = jnp.bfloat16
F32 = jnp.float32


def aggregate(dsts, srcs, count, feats, weights, nfeat):
    fcols, nsrc = feats.shape
    slots = weights.shape[0]
    dtiles = nsrc // TILE // 2
    per_owner = dtiles // nfeat
    parts = 4
    owners = nfeat // parts

    def kernel(dst, src, cnt, x_ref, w_hbm, o_hbm, acc, out, buf, sem_w, sem_o):
        steps = pl.cdiv(cnt[0], SLOTS_STEP)

        def fetch(i):
            place = lax.rem(i, BUFFERS)
            return pltpu.make_async_copy(
                w_hbm.at[pl.ds(i * SLOTS_STEP, SLOTS_STEP)], buf.at[place], sem_w.at[place]
            )

        for i in range(BUFFERS - 1):

            @pl.when(i < steps)
            def _():
                fetch(i).start()

        acc[...] = jnp.zeros_like(acc)
        zero = jnp.zeros((fcols, TILE), BF16)

        def source(slot):
            return x_ref[:, pl.ds(pl.multiple_of(src[slot] * TILE, TILE), TILE)]

        def step(i, carry):
            @pl.when(i + BUFFERS - 1 < steps)
            def _():
                fetch(i + BUFFERS - 1).start()

            fetch(i).wait()
            w_ref = buf.at[lax.rem(i, BUFFERS)]
            first = i * SLOTS_STEP
            products = []
            for u in range(0, SLOTS_STEP, 2):
                left = jnp.concatenate(
                    [
                        jnp.concatenate([source(first + u), zero], 1),
                        jnp.concatenate([zero, source(first + u + 1)], 1),
                    ],
                    0,
                )
                right = jnp.concatenate([w_ref[u], w_ref[u + 1]], 1)
                both = lax.dot_general(left, right, (((1,), (1,)), ((), ())), preferred_element_type=F32)
                products += [both[:fcols], both[fcols:]]
            for u in range(SLOTS_STEP):
                acc[dst[first + u]] += jnp.where(first + u < cnt[0], products[u], 0.0)
            return carry

        lax.fori_loop(0, steps, step, 0)
        put = []
        for p in range(parts):
            tiles = acc[p * owners * per_owner : (p + 1) * owners * per_owner]
            out[p * owners : (p + 1) * owners] = tiles.reshape(owners, per_owner * fcols, TILE).astype(BF16)
            put.append(
                pltpu.make_async_copy(
                    out.at[pl.ds(p * owners, owners)], o_hbm.at[pl.ds(p * owners, owners)], sem_o.at[p]
                )
            )
            put[-1].start()
        for c in put:
            c.wait()

    shape = (nfeat, per_owner * fcols, TILE)
    return pl.pallas_call(
        kernel,
        in_specs=[pl.BlockSpec(memory_space=pltpu.SMEM)] * 3
        + [pl.BlockSpec(memory_space=pltpu.VMEM), pl.BlockSpec(memory_space=pl.ANY)],
        out_specs=pl.BlockSpec(memory_space=pl.ANY),
        scratch_shapes=[
            pltpu.VMEM((dtiles, fcols, TILE), F32),
            pltpu.VMEM(shape, BF16),
            pltpu.VMEM((BUFFERS, SLOTS_STEP, TILE, TILE), BF16),
            pltpu.SemaphoreType.DMA((BUFFERS,)),
            pltpu.SemaphoreType.DMA((parts,)),
        ],
        out_shape=jax.ShapeDtypeStruct(shape, BF16),
        name="aggregate",
        compiler_params=pltpu.CompilerParams(vmem_limit_bytes=56 << 20),
        cost_estimate=pl.CostEstimate(
            flops=2 * slots * fcols * TILE * TILE,
            bytes_accessed=slots * TILE * TILE * 2 + fcols * nsrc * 2,
            transcendentals=0,
        ),
    )(dsts, srcs, count, feats, weights)


def contract_rows(a, b):
    return lax.dot_general(a, b, (((0,), (0,)), ((), ())), preferred_element_type=F32)


def in_vmem(n):
    return [pl.BlockSpec(memory_space=pltpu.VMEM)] * n


def pack(place, feats, w_self, w_neigh, nfeat, rows_dev):
    fcols = feats.shape[0]
    hid = w_self.shape[1]
    per_owner = rows_dev // TILE
    share = fcols // 2
    part_rows = share // 2
    parts = 4
    owners = nfeat // parts

    def kernel(at, x_hbm, ws_hbm, wn_hbm, o_hbm, x_ref, o_ref, both, sem_x, sem_o, sem_w):
        get_w = [
            pltpu.make_async_copy(ws_hbm, both.at[:, pl.ds(0, hid)], sem_w.at[0]),
            pltpu.make_async_copy(wn_hbm, both.at[:, pl.ds(hid, hid)], sem_w.at[1]),
        ]
        width = owners * rows_dev
        get_x = [
            pltpu.make_async_copy(
                x_hbm.at[:, pl.ds(p * width, width)], x_ref.at[:, pl.ds(p * width, width)], sem_x.at[p]
            )
            for p in range(parts)
        ]
        put = [
            pltpu.make_async_copy(
                o_ref.at[pl.ds(p * owners, owners)], o_hbm.at[pl.ds(p * owners, owners)], sem_o.at[p]
            )
            for p in range(parts)
        ]
        for c in get_w + get_x:
            c.start()
        for c in get_w:
            c.wait()
        core, x = lax.rem(at[0], 2), lax.div(at[0], 2)
        piece = both[pl.ds(pl.multiple_of(core * share, share), share), pl.ds(pl.multiple_of(x * TILE, TILE), TILE)]
        for p in range(parts):
            get_x[p].wait()
            for c in range(p * owners, (p + 1) * owners):
                for q in range(per_owner):
                    tile = c * per_owner + q
                    o_ref[c, q * fcols : (q + 1) * fcols, :] = x_ref[:, tile * TILE : (tile + 1) * TILE]
                first = c % 2 * part_rows
                o_ref[c, per_owner * fcols :, :] = piece[first : first + part_rows]
            put[p].start()
        for c in put:
            c.wait()

    out = (nfeat, per_owner * fcols + part_rows, TILE)
    return pl.pallas_call(
        kernel,
        in_specs=[pl.BlockSpec(memory_space=pltpu.SMEM)] + [pl.BlockSpec(memory_space=pl.ANY)] * 3,
        out_specs=pl.BlockSpec(memory_space=pl.ANY),
        out_shape=jax.ShapeDtypeStruct(out, BF16),
        scratch_shapes=[
            pltpu.VMEM((fcols, nfeat * rows_dev), BF16),
            pltpu.VMEM(out, BF16),
            pltpu.VMEM((fcols, 2 * hid), BF16),
            pltpu.SemaphoreType.DMA((parts,)),
            pltpu.SemaphoreType.DMA((parts,)),
            pltpu.SemaphoreType.DMA((2,)),
        ],
        name="pack",
        compiler_params=pltpu.CompilerParams(vmem_limit_bytes=60 << 20),
        cost_estimate=pl.CostEstimate(flops=0, bytes_accessed=3 << 20, transcendentals=0),
    )(place, feats, w_self, w_neigh)


def contract_rows(a, b):
    return lax.dot_general(a, b, (((0,), (0,)), ((), ())), preferred_element_type=F32)


def row_tile(ref, q, fcols):
    return ref[:, q * fcols : (q + 1) * fcols, :].reshape(ref.shape[0] * fcols, TILE)


def own_part(place, same_core, other_core, x_rows, bias, tiles):
    nx, nfeat, share, _ = same_core.shape
    hid = bias.shape[1]
    fcols = 2 * share

    def kernel(at, w0, w1, x_ref, b_ref, pre_ref, wn_ref, both):
        for k in range(nx):
            x = lax.bitwise_xor(lax.div(at[0], 2), k)
            lanes = pl.ds(pl.multiple_of(x * TILE, TILE), TILE)
            for r, ref in enumerate((w0, w1)):
                core = lax.bitwise_xor(lax.rem(at[0], 2), r)
                both[:, pl.ds(pl.multiple_of(core * share, share), share), lanes] = ref[k]
        ws = both[:, :, :hid].reshape(nfeat * fcols, hid)
        wn_ref[...] = both[:, :, hid:].reshape(nfeat * fcols, hid)
        for q in range(tiles):
            pre_ref[q] = contract_rows(row_tile(x_ref, q, fcols), ws) + b_ref[...]

    return pl.pallas_call(
        kernel,
        in_specs=[pl.BlockSpec(memory_space=pltpu.SMEM)] + in_vmem(4),
        out_specs=in_vmem(2),
        out_shape=[
            jax.ShapeDtypeStruct((tiles, TILE, hid), F32),
            jax.ShapeDtypeStruct((nfeat * fcols, hid), BF16),
        ],
        scratch_shapes=[pltpu.VMEM((nfeat, fcols, 2 * hid), BF16)],
        name="own_part",
        compiler_params=pltpu.CompilerParams(vmem_limit_bytes=16 << 20),
        cost_estimate=pl.CostEstimate(
            flops=2 * nfeat * fcols * tiles * TILE * hid, bytes_accessed=4 << 20, transcendentals=0
        ),
    )(place, same_core, other_core, x_rows, bias)


def layer(place, pre_own, a_rows, w_neigh, x_rows, upstream):
    nfeat = x_rows.shape[0]
    feats, hid = w_neigh.shape
    fcols = feats // nfeat
    rows = upstream.shape[0]
    tiles = rows // TILE
    halves = hid // TILE
    out_rows = halves * fcols + 8

    def kernel(at, pre, a_ref, wn, x_ref, up_ref, hid_ref, g_ref, deltas):
        gb = jnp.zeros((1, hid), F32)
        for q in range(tiles):
            here = slice(q * TILE, (q + 1) * TILE)
            v = pre[q] + contract_rows(row_tile(a_ref, q, fcols), wn[...])
            sq = v * v
            t = jnp.tanh(GELU_A * (v + GELU_B * sq * v))
            half = 0.5 * (1.0 + t)
            hid_ref[here, :] = (v * half).astype(BF16)
            slope = half + 0.5 * v * (1.0 - t * t) * (GELU_A * (1.0 + 3.0 * GELU_B * sq))
            delta = (up_ref[here, :].astype(F32) * slope).astype(BF16)
            deltas[here, :] = delta
            gb = gb + jnp.sum(delta.astype(F32), axis=0, keepdims=True)
        core = lax.rem(at[0], 2)
        for slot, ref in ((core, x_ref), (1 - core, a_ref)):
            left = jnp.concatenate([row_tile(ref, q, fcols) for q in range(tiles)], axis=1)
            grad = jnp.dot(left, deltas[...], preferred_element_type=F32).astype(BF16)
            for h in range(halves):
                g_ref[slot, :, h * fcols : (h + 1) * fcols, :] = grad[:, h * TILE : (h + 1) * TILE].reshape(
                    nfeat, fcols, TILE
                )
        high = gb.astype(BF16).astype(F32)
        mid = (gb - high).astype(BF16).astype(F32)
        low = gb - high - mid
        lines = [part[:, h * TILE : (h + 1) * TILE] for part in (high, mid, low) for h in range(halves)]
        lines = jnp.concatenate(lines + [jnp.zeros((8 - len(lines), TILE), F32)], axis=0).astype(BF16)
        g_ref[0, :, halves * fcols :, :] = jnp.broadcast_to(lines[None], (nfeat, 8, TILE))
        g_ref[1, :, halves * fcols :, :] = jnp.zeros((nfeat, 8, TILE), BF16)

    return pl.pallas_call(
        kernel,
        in_specs=[pl.BlockSpec(memory_space=pltpu.SMEM)] + in_vmem(5),
        out_specs=in_vmem(2),
        out_shape=[
            jax.ShapeDtypeStruct((rows, hid), BF16),
            jax.ShapeDtypeStruct((2, nfeat, out_rows, TILE), BF16),
        ],
        scratch_shapes=[pltpu.VMEM((rows, hid), BF16)],
        name="layer",
        compiler_params=pltpu.CompilerParams(vmem_limit_bytes=24 << 20),
        cost_estimate=pl.CostEstimate(
            flops=6 * feats * rows * hid, bytes_accessed=6 << 20, transcendentals=rows * hid
        ),
    )(place, pre_own, a_rows, w_neigh, x_rows, upstream)


def finish(place, mine, other, fcols):
    halves = (mine.shape[0] - 8) // fcols
    hid = halves * TILE

    def kernel(at, m_ref, o_ref, gs_ref, gn_ref, gb_ref):
        first = lax.rem(at[0], 2) == 0
        for h in range(halves):
            lanes, rows = slice(h * TILE, (h + 1) * TILE), slice(h * fcols, (h + 1) * fcols)
            gs_ref[:, lanes] = jnp.where(first, m_ref[rows], o_ref[rows])
            gn_ref[:, lanes] = jnp.where(first, o_ref[rows], m_ref[rows])
        both = m_ref[halves * fcols :] + o_ref[halves * fcols :]
        for h in range(halves):
            parts = [both[halves * p + h : halves * p + h + 1] for p in range(3)]
            gb_ref[:, h * TILE : (h + 1) * TILE] = parts[0] + parts[1] + parts[2]

    return pl.pallas_call(
        kernel,
        in_specs=[pl.BlockSpec(memory_space=pltpu.SMEM)] + in_vmem(2),
        out_specs=in_vmem(3),
        out_shape=[
            jax.ShapeDtypeStruct((fcols, hid), F32),
            jax.ShapeDtypeStruct((fcols, hid), F32),
            jax.ShapeDtypeStruct((1, hid), F32),
        ],
        name="finish",
        compiler_params=pltpu.CompilerParams(vmem_limit_bytes=8 << 20),
    )(place, mine, other)


def body(features_t, tile_weights, tile_dst, tile_src, tile_count, w_self, w_neigh, bias, grad_hidden):
    feats = features_t[0]
    fcols = feats.shape[0]
    nv = lax.axis_size("vgroup")
    nfeat = lax.axis_size("feat")
    rows_dev, hid = grad_hidden.shape
    tiles = rows_dev // TILE
    place = lax.axis_index("vgroup")[None].astype(jnp.int32)

    def direct(value, bits):
        return [lax.ppermute(value, "vgroup", [(a, a ^ bit) for a in range(nv)]) for bit in bits]

    with jax.named_scope("send_features"):
        outgoing = pack(place, feats, w_self, w_neigh, nfeat, rows_dev)
        x_rows = lax.all_to_all(outgoing, "feat", 0, 0, tiled=True)

    agg = aggregate(tile_dst[0], tile_src[0], tile_count, feats, tile_weights[0], nfeat)
    x_rows, agg = lax.optimization_barrier((x_rows, agg))
    with jax.named_scope("send_aggregated"):
        a_rows = lax.all_to_all(agg, "feat", 0, 0, tiled=True)

    with jax.named_scope("weights_over_vgroup"):
        part = x_rows[:, tiles * fcols :, :]
        other = lax.ppermute(part, "feat", [(a, a ^ 1) for a in range(nfeat)])
        even = lax.axis_index("feat") % 2 == 0
        piece = jnp.concatenate([jnp.where(even, part, other), jnp.where(even, other, part)], axis=1)
        same_core = jnp.stack([piece] + direct(piece, (2, 4, 6)))
        [other_core] = direct(same_core, (1,))

    pre_own, wn = own_part(place, same_core, other_core, x_rows, bias[None, :], tiles)
    hidden, grads = layer(place, pre_own, a_rows, wn, x_rows, grad_hidden)

    with jax.named_scope("reduce_grads"):
        [got] = direct(grads[1], (1,))
        pair = (grads[0].astype(F32) + got.astype(F32)).astype(BF16)
        arrived = lax.all_to_all(pair, "feat", 0, 0, tiled=True)
        total = jnp.sum(arrived.astype(F32), axis=0)
        total = sum(direct(total, (2, 4, 6)), total)
        [other] = direct(total, (1,))
        grad_self, grad_neigh, grad_bias = finish(place, total, other, fcols)
    return (hidden, grad_self, grad_neigh, grad_bias[0])


def solution(mesh):
    return jax.shard_map(
        body,
        mesh=mesh,
        in_specs=(
            P("vgroup", "feat", None),
            P("vgroup", None, None, None),
            P("vgroup", None),
            P("vgroup", None),
            P("vgroup"),
            P("feat", None),
            P("feat", None),
            P(),
            P(("vgroup", "feat"), None),
        ),
        out_specs=(P(("vgroup", "feat"), None), P("feat", None), P("feat", None), P()),
        check_vma=False,
    )
```

```python
import jax
import jax.numpy as jnp
from jax import lax
from jax.experimental import pallas as pl
from jax.experimental.pallas import tpu as pltpu
from jax.sharding import PartitionSpec as P

TILE = 128
SLOTS_STEP = 64
BUFFERS = 4
GELU_A = 0.7978845608
GELU_B = 0.044715
BF16 = jnp.bfloat16
F32 = jnp.float32


def aggregate(dsts, srcs, count, feats, weights, nfeat):
    fcols, nsrc = feats.shape
    slots = weights.shape[0]
    dtiles = nsrc // TILE // 2
    per_owner = dtiles // nfeat
    parts = 4
    owners = nfeat // parts

    def kernel(dst, src, cnt, x_ref, w_hbm, o_hbm, acc, out, buf, sem_w, sem_o):
        steps = pl.cdiv(cnt[0], SLOTS_STEP)

        def fetch(i):
            place = lax.rem(i, BUFFERS)
            return pltpu.make_async_copy(
                w_hbm.at[pl.ds(i * SLOTS_STEP, SLOTS_STEP)], buf.at[place], sem_w.at[place]
            )

        for i in range(BUFFERS - 1):

            @pl.when(i < steps)
            def _():
                fetch(i).start()

        acc[...] = jnp.zeros_like(acc)
        zero = jnp.zeros((fcols, TILE), BF16)

        def source(slot):
            return x_ref[:, pl.ds(pl.multiple_of(src[slot] * TILE, TILE), TILE)]

        def step(i, carry):
            @pl.when(i + BUFFERS - 1 < steps)
            def _():
                fetch(i + BUFFERS - 1).start()

            fetch(i).wait()
            w_ref = buf.at[lax.rem(i, BUFFERS)]
            first = i * SLOTS_STEP
            products = []
            for u in range(0, SLOTS_STEP, 2):
                left = jnp.concatenate(
                    [
                        jnp.concatenate([source(first + u), zero], 1),
                        jnp.concatenate([zero, source(first + u + 1)], 1),
                    ],
                    0,
                )
                right = jnp.concatenate([w_ref[u], w_ref[u + 1]], 1)
                both = lax.dot_general(left, right, (((1,), (1,)), ((), ())), preferred_element_type=F32)
                products += [both[:fcols], both[fcols:]]
            for u in range(SLOTS_STEP):
                acc[dst[first + u]] += jnp.where(first + u < cnt[0], products[u], 0.0)
            return carry

        lax.fori_loop(0, steps, step, 0)
        put = []
        for p in range(parts):
            tiles = acc[p * owners * per_owner : (p + 1) * owners * per_owner]
            out[p * owners : (p + 1) * owners] = tiles.reshape(owners, per_owner * fcols, TILE).astype(BF16)
            put.append(
                pltpu.make_async_copy(
                    out.at[pl.ds(p * owners, owners)], o_hbm.at[pl.ds(p * owners, owners)], sem_o.at[p]
                )
            )
            put[-1].start()
        for c in put:
            c.wait()

    shape = (nfeat, per_owner * fcols, TILE)
    return pl.pallas_call(
        kernel,
        in_specs=[pl.BlockSpec(memory_space=pltpu.SMEM)] * 3
        + [pl.BlockSpec(memory_space=pltpu.VMEM), pl.BlockSpec(memory_space=pl.ANY)],
        out_specs=pl.BlockSpec(memory_space=pl.ANY),
        scratch_shapes=[
            pltpu.VMEM((dtiles, fcols, TILE), F32),
            pltpu.VMEM(shape, BF16),
            pltpu.VMEM((BUFFERS, SLOTS_STEP, TILE, TILE), BF16),
            pltpu.SemaphoreType.DMA((BUFFERS,)),
            pltpu.SemaphoreType.DMA((parts,)),
        ],
        out_shape=jax.ShapeDtypeStruct(shape, BF16),
        name="aggregate",
        compiler_params=pltpu.CompilerParams(vmem_limit_bytes=56 << 20),
        cost_estimate=pl.CostEstimate(
            flops=2 * slots * fcols * TILE * TILE,
            bytes_accessed=slots * TILE * TILE * 2 + fcols * nsrc * 2,
            transcendentals=0,
        ),
    )(dsts, srcs, count, feats, weights)


def contract_rows(a, b):
    return lax.dot_general(a, b, (((0,), (0,)), ((), ())), preferred_element_type=F32)


def in_vmem(n):
    return [pl.BlockSpec(memory_space=pltpu.VMEM)] * n


def pack(place, feats, w_self, w_neigh, nfeat, rows_dev):
    fcols = feats.shape[0]
    hid = w_self.shape[1]
    per_owner = rows_dev // TILE
    share = fcols // 2
    part_rows = share // 2
    parts = 4
    owners = nfeat // parts

    def kernel(at, x_hbm, ws_hbm, wn_hbm, o_hbm, x_ref, o_ref, both, sem_x, sem_o, sem_w):
        get_w = [
            pltpu.make_async_copy(ws_hbm, both.at[:, pl.ds(0, hid)], sem_w.at[0]),
            pltpu.make_async_copy(wn_hbm, both.at[:, pl.ds(hid, hid)], sem_w.at[1]),
        ]
        width = owners * rows_dev
        get_x = [
            pltpu.make_async_copy(
                x_hbm.at[:, pl.ds(p * width, width)], x_ref.at[:, pl.ds(p * width, width)], sem_x.at[p]
            )
            for p in range(parts)
        ]
        put = [
            pltpu.make_async_copy(
                o_ref.at[pl.ds(p * owners, owners)], o_hbm.at[pl.ds(p * owners, owners)], sem_o.at[p]
            )
            for p in range(parts)
        ]
        for c in get_w + get_x:
            c.start()
        for c in get_w:
            c.wait()
        core, x = lax.rem(at[0], 2), lax.div(at[0], 2)
        piece = both[pl.ds(pl.multiple_of(core * share, share), share), pl.ds(pl.multiple_of(x * TILE, TILE), TILE)]
        for p in range(parts):
            get_x[p].wait()
            for c in range(p * owners, (p + 1) * owners):
                for q in range(per_owner):
                    tile = c * per_owner + q
                    o_ref[c, q * fcols : (q + 1) * fcols, :] = x_ref[:, tile * TILE : (tile + 1) * TILE]
                first = c % 2 * part_rows
                o_ref[c, per_owner * fcols :, :] = piece[first : first + part_rows]
            put[p].start()
        for c in put:
            c.wait()

    out = (nfeat, per_owner * fcols + part_rows, TILE)
    return pl.pallas_call(
        kernel,
        in_specs=[pl.BlockSpec(memory_space=pltpu.SMEM)] + [pl.BlockSpec(memory_space=pl.ANY)] * 3,
        out_specs=pl.BlockSpec(memory_space=pl.ANY),
        out_shape=jax.ShapeDtypeStruct(out, BF16),
        scratch_shapes=[
            pltpu.VMEM((fcols, nfeat * rows_dev), BF16),
            pltpu.VMEM(out, BF16),
            pltpu.VMEM((fcols, 2 * hid), BF16),
            pltpu.SemaphoreType.DMA((parts,)),
            pltpu.SemaphoreType.DMA((parts,)),
            pltpu.SemaphoreType.DMA((2,)),
        ],
        name="pack",
        compiler_params=pltpu.CompilerParams(vmem_limit_bytes=60 << 20),
        cost_estimate=pl.CostEstimate(flops=0, bytes_accessed=3 << 20, transcendentals=0),
    )(place, feats, w_self, w_neigh)


def contract_rows(a, b):
    return lax.dot_general(a, b, (((0,), (0,)), ((), ())), preferred_element_type=F32)


def row_tile(ref, q, fcols):
    return ref[:, q * fcols : (q + 1) * fcols, :].reshape(ref.shape[0] * fcols, TILE)


def own_part(place, same_core, other_core, x_rows, bias, tiles):
    nx, nfeat, share, _ = same_core.shape
    hid = bias.shape[1]
    fcols = 2 * share

    def kernel(at, w0, w1, x_ref, b_ref, pre_ref, wn_ref, both):
        for k in range(nx):
            x = lax.bitwise_xor(lax.div(at[0], 2), k)
            lanes = pl.ds(pl.multiple_of(x * TILE, TILE), TILE)
            for r, ref in enumerate((w0, w1)):
                core = lax.bitwise_xor(lax.rem(at[0], 2), r)
                both[:, pl.ds(pl.multiple_of(core * share, share), share), lanes] = ref[k]
        ws = both[:, :, :hid].reshape(nfeat * fcols, hid)
        wn_ref[...] = both[:, :, hid:].reshape(nfeat * fcols, hid)
        for q in range(tiles):
            pre_ref[q] = contract_rows(row_tile(x_ref, q, fcols), ws) + b_ref[...]

    return pl.pallas_call(
        kernel,
        in_specs=[pl.BlockSpec(memory_space=pltpu.SMEM)] + in_vmem(4),
        out_specs=in_vmem(2),
        out_shape=[
            jax.ShapeDtypeStruct((tiles, TILE, hid), F32),
            jax.ShapeDtypeStruct((nfeat * fcols, hid), BF16),
        ],
        scratch_shapes=[pltpu.VMEM((nfeat, fcols, 2 * hid), BF16)],
        name="own_part",
        compiler_params=pltpu.CompilerParams(vmem_limit_bytes=16 << 20),
        cost_estimate=pl.CostEstimate(
            flops=2 * nfeat * fcols * tiles * TILE * hid, bytes_accessed=4 << 20, transcendentals=0
        ),
    )(place, same_core, other_core, x_rows, bias)


def layer(place, pre_own, a_rows, w_neigh, x_rows, upstream):
    nfeat = x_rows.shape[0]
    feats, hid = w_neigh.shape
    fcols = feats // nfeat
    rows = upstream.shape[0]
    tiles = rows // TILE
    halves = hid // TILE
    out_rows = halves * fcols + 8

    def kernel(at, pre, a_ref, wn, x_ref, up_ref, hid_ref, g_ref, deltas):
        gb = jnp.zeros((1, hid), F32)
        for q in range(tiles):
            here = slice(q * TILE, (q + 1) * TILE)
            v = pre[q] + contract_rows(row_tile(a_ref, q, fcols), wn[...])
            sq = v * v
            t = jnp.tanh(GELU_A * (v + GELU_B * sq * v))
            half = 0.5 * (1.0 + t)
            hid_ref[here, :] = (v * half).astype(BF16)
            slope = half + 0.5 * v * (1.0 - t * t) * (GELU_A * (1.0 + 3.0 * GELU_B * sq))
            delta = (up_ref[here, :].astype(F32) * slope).astype(BF16)
            deltas[here, :] = delta
            gb = gb + jnp.sum(delta.astype(F32), axis=0, keepdims=True)
        core = lax.rem(at[0], 2)
        for slot, ref in ((core, x_ref), (1 - core, a_ref)):
            left = jnp.concatenate([row_tile(ref, q, fcols) for q in range(tiles)], axis=1)
            grad = jnp.dot(left, deltas[...], preferred_element_type=F32).astype(BF16)
            for h in range(halves):
                g_ref[slot, :, h * fcols : (h + 1) * fcols, :] = grad[:, h * TILE : (h + 1) * TILE].reshape(
                    nfeat, fcols, TILE
                )
        high = gb.astype(BF16).astype(F32)
        mid = (gb - high).astype(BF16).astype(F32)
        low = gb - high - mid
        lines = [part[:, h * TILE : (h + 1) * TILE] for part in (high, mid, low) for h in range(halves)]
        lines = jnp.concatenate(lines + [jnp.zeros((8 - len(lines), TILE), F32)], axis=0).astype(BF16)
        g_ref[0, :, halves * fcols :, :] = jnp.broadcast_to(lines[None], (nfeat, 8, TILE))
        g_ref[1, :, halves * fcols :, :] = jnp.zeros((nfeat, 8, TILE), BF16)

    return pl.pallas_call(
        kernel,
        in_specs=[pl.BlockSpec(memory_space=pltpu.SMEM)] + in_vmem(5),
        out_specs=in_vmem(2),
        out_shape=[
            jax.ShapeDtypeStruct((rows, hid), BF16),
            jax.ShapeDtypeStruct((2, nfeat, out_rows, TILE), BF16),
        ],
        scratch_shapes=[pltpu.VMEM((rows, hid), BF16)],
        name="layer",
        compiler_params=pltpu.CompilerParams(vmem_limit_bytes=24 << 20),
        cost_estimate=pl.CostEstimate(
            flops=6 * feats * rows * hid, bytes_accessed=6 << 20, transcendentals=rows * hid
        ),
    )(place, pre_own, a_rows, w_neigh, x_rows, upstream)


def finish(place, mine, other, fcols):
    halves = (mine.shape[0] - 8) // fcols
    hid = halves * TILE

    def kernel(at, m_ref, o_ref, gs_ref, gn_ref, gb_ref):
        first = lax.rem(at[0], 2) == 0
        for h in range(halves):
            lanes, rows = slice(h * TILE, (h + 1) * TILE), slice(h * fcols, (h + 1) * fcols)
            gs_ref[:, lanes] = jnp.where(first, m_ref[rows], o_ref[rows])
            gn_ref[:, lanes] = jnp.where(first, o_ref[rows], m_ref[rows])
        both = m_ref[halves * fcols :] + o_ref[halves * fcols :]
        for h in range(halves):
            parts = [both[halves * p + h : halves * p + h + 1] for p in range(3)]
            gb_ref[:, h * TILE : (h + 1) * TILE] = parts[0] + parts[1] + parts[2]

    return pl.pallas_call(
        kernel,
        in_specs=[pl.BlockSpec(memory_space=pltpu.SMEM)] + in_vmem(2),
        out_specs=in_vmem(3),
        out_shape=[
            jax.ShapeDtypeStruct((fcols, hid), F32),
            jax.ShapeDtypeStruct((fcols, hid), F32),
            jax.ShapeDtypeStruct((1, hid), F32),
        ],
        name="finish",
        compiler_params=pltpu.CompilerParams(vmem_limit_bytes=8 << 20),
    )(place, mine, other)


def body(features_t, tile_weights, tile_dst, tile_src, tile_count, w_self, w_neigh, bias, grad_hidden):
    feats = features_t[0]
    fcols = feats.shape[0]
    nv = lax.axis_size("vgroup")
    nfeat = lax.axis_size("feat")
    rows_dev, hid = grad_hidden.shape
    tiles = rows_dev // TILE
    place = lax.axis_index("vgroup")[None].astype(jnp.int32)

    def direct(value, bits):
        return [lax.ppermute(value, "vgroup", [(a, a ^ bit) for a in range(nv)]) for bit in bits]

    with jax.named_scope("send_features"):
        outgoing = pack(place, feats, w_self, w_neigh, nfeat, rows_dev)
        x_rows = lax.all_to_all(outgoing, "feat", 0, 0, tiled=True)

    agg = aggregate(tile_dst[0], tile_src[0], tile_count, feats, tile_weights[0], nfeat)
    x_rows, agg = lax.optimization_barrier((x_rows, agg))
    with jax.named_scope("send_aggregated"):
        a_rows = lax.all_to_all(agg, "feat", 0, 0, tiled=True)

    with jax.named_scope("weights_over_vgroup"):
        part = x_rows[:, tiles * fcols :, :]
        other = lax.ppermute(part, "feat", [(a, a ^ 1) for a in range(nfeat)])
        even = lax.axis_index("feat") % 2 == 0
        piece = jnp.concatenate([jnp.where(even, part, other), jnp.where(even, other, part)], axis=1)
        same_core = jnp.stack([piece] + direct(piece, (2, 4, 6)))
        [other_core] = direct(same_core, (1,))

    pre_own, wn = own_part(place, same_core, other_core, x_rows, bias[None, :], tiles)
    hidden, grads = layer(place, pre_own, a_rows, wn, x_rows, grad_hidden)

    with jax.named_scope("reduce_grads"):
        [got] = direct(grads[1], (1,))
        pair = (grads[0].astype(F32) + got.astype(F32)).astype(BF16)
        arrived = lax.all_to_all(pair, "feat", 0, 0, tiled=True)
        total = jnp.sum(arrived.astype(F32), axis=0)
        total = sum(direct(total, (2, 6, 4)), total)
        [other] = direct(total, (1,))
        grad_self, grad_neigh, grad_bias = finish(place, total, other, fcols)
    return (hidden, grad_self, grad_neigh, grad_bias[0])


def solution(mesh):
    return jax.shard_map(
        body,
        mesh=mesh,
        in_specs=(
            P("vgroup", "feat", None),
            P("vgroup", None, None, None),
            P("vgroup", None),
            P("vgroup", None),
            P("vgroup"),
            P("feat", None),
            P("feat", None),
            P(),
            P(("vgroup", "feat"), None),
        ),
        out_specs=(P(("vgroup", "feat"), None), P("feat", None), P("feat", None), P()),
        check_vma=False,
    )
```

```python
import jax
import jax.numpy as jnp
from jax import lax
from jax.experimental import pallas as pl
from jax.experimental.pallas import tpu as pltpu
from jax.sharding import PartitionSpec as P

TILE = 128
SLOTS_STEP = 64
BUFFERS = 4
GELU_A = 0.7978845608
GELU_B = 0.044715
BF16 = jnp.bfloat16
F32 = jnp.float32


def aggregate(dsts, srcs, count, feats, weights, nfeat):
    fcols, nsrc = feats.shape
    slots = weights.shape[0]
    dtiles = nsrc // TILE // 2
    per_owner = dtiles // nfeat
    parts = 4
    owners = nfeat // parts

    def kernel(dst, src, cnt, x_ref, w_hbm, o_hbm, acc, out, buf, sem_w, sem_o):
        steps = pl.cdiv(cnt[0], SLOTS_STEP)

        def fetch(i):
            place = lax.rem(i, BUFFERS)
            return pltpu.make_async_copy(
                w_hbm.at[pl.ds(i * SLOTS_STEP, SLOTS_STEP)], buf.at[place], sem_w.at[place]
            )

        for i in range(BUFFERS - 1):

            @pl.when(i < steps)
            def _():
                fetch(i).start()

        acc[...] = jnp.zeros_like(acc)
        zero = jnp.zeros((fcols, TILE), BF16)

        def source(slot):
            return x_ref[:, pl.ds(pl.multiple_of(src[slot] * TILE, TILE), TILE)]

        def step(i, carry):
            @pl.when(i + BUFFERS - 1 < steps)
            def _():
                fetch(i + BUFFERS - 1).start()

            fetch(i).wait()
            w_ref = buf.at[lax.rem(i, BUFFERS)]
            first = i * SLOTS_STEP
            products = []
            for u in range(0, SLOTS_STEP, 2):
                left = jnp.concatenate(
                    [
                        jnp.concatenate([source(first + u), zero], 1),
                        jnp.concatenate([zero, source(first + u + 1)], 1),
                    ],
                    0,
                )
                right = jnp.concatenate([w_ref[u], w_ref[u + 1]], 1)
                both = lax.dot_general(left, right, (((1,), (1,)), ((), ())), preferred_element_type=F32)
                products += [both[:fcols], both[fcols:]]
            for u in range(SLOTS_STEP):
                acc[dst[first + u]] += jnp.where(first + u < cnt[0], products[u], 0.0)
            return carry

        lax.fori_loop(0, steps, step, 0)
        put = []
        for p in range(parts):
            tiles = acc[p * owners * per_owner : (p + 1) * owners * per_owner]
            out[p * owners : (p + 1) * owners] = tiles.reshape(owners, per_owner * fcols, TILE).astype(BF16)
            put.append(
                pltpu.make_async_copy(
                    out.at[pl.ds(p * owners, owners)], o_hbm.at[pl.ds(p * owners, owners)], sem_o.at[p]
                )
            )
            put[-1].start()
        for c in put:
            c.wait()

    shape = (nfeat, per_owner * fcols, TILE)
    return pl.pallas_call(
        kernel,
        in_specs=[pl.BlockSpec(memory_space=pltpu.SMEM)] * 3
        + [pl.BlockSpec(memory_space=pltpu.VMEM), pl.BlockSpec(memory_space=pl.ANY)],
        out_specs=pl.BlockSpec(memory_space=pl.ANY),
        scratch_shapes=[
            pltpu.VMEM((dtiles, fcols, TILE), F32),
            pltpu.VMEM(shape, BF16),
            pltpu.VMEM((BUFFERS, SLOTS_STEP, TILE, TILE), BF16),
            pltpu.SemaphoreType.DMA((BUFFERS,)),
            pltpu.SemaphoreType.DMA((parts,)),
        ],
        out_shape=jax.ShapeDtypeStruct(shape, BF16),
        name="aggregate",
        compiler_params=pltpu.CompilerParams(vmem_limit_bytes=56 << 20),
        cost_estimate=pl.CostEstimate(
            flops=2 * slots * fcols * TILE * TILE,
            bytes_accessed=slots * TILE * TILE * 2 + fcols * nsrc * 2,
            transcendentals=0,
        ),
    )(dsts, srcs, count, feats, weights)


def contract_rows(a, b):
    return lax.dot_general(a, b, (((0,), (0,)), ((), ())), preferred_element_type=F32)


def in_vmem(n):
    return [pl.BlockSpec(memory_space=pltpu.VMEM)] * n


def pack(place, feats, w_self, w_neigh, nfeat, rows_dev):
    fcols = feats.shape[0]
    hid = w_self.shape[1]
    per_owner = rows_dev // TILE
    share = fcols // 2
    part_rows = share // 2
    parts = 4
    owners = nfeat // parts

    def kernel(at, x_hbm, ws_hbm, wn_hbm, o_hbm, x_ref, o_ref, both, sem_x, sem_o, sem_w):
        get_w = [
            pltpu.make_async_copy(ws_hbm, both.at[:, pl.ds(0, hid)], sem_w.at[0]),
            pltpu.make_async_copy(wn_hbm, both.at[:, pl.ds(hid, hid)], sem_w.at[1]),
        ]
        width = owners * rows_dev
        get_x = [
            pltpu.make_async_copy(
                x_hbm.at[:, pl.ds(p * width, width)], x_ref.at[:, pl.ds(p * width, width)], sem_x.at[p]
            )
            for p in range(parts)
        ]
        put = [
            pltpu.make_async_copy(
                o_ref.at[pl.ds(p * owners, owners)], o_hbm.at[pl.ds(p * owners, owners)], sem_o.at[p]
            )
            for p in range(parts)
        ]
        for c in get_w + get_x:
            c.start()
        for c in get_w:
            c.wait()
        core, x = lax.rem(at[0], 2), lax.div(at[0], 2)
        piece = both[pl.ds(pl.multiple_of(core * share, share), share), pl.ds(pl.multiple_of(x * TILE, TILE), TILE)]
        for p in range(parts):
            get_x[p].wait()
            for c in range(p * owners, (p + 1) * owners):
                for q in range(per_owner):
                    tile = c * per_owner + q
                    o_ref[c, q * fcols : (q + 1) * fcols, :] = x_ref[:, tile * TILE : (tile + 1) * TILE]
                first = c % 2 * part_rows
                o_ref[c, per_owner * fcols :, :] = piece[first : first + part_rows]
            put[p].start()
        for c in put:
            c.wait()

    out = (nfeat, per_owner * fcols + part_rows, TILE)
    return pl.pallas_call(
        kernel,
        in_specs=[pl.BlockSpec(memory_space=pltpu.SMEM)] + [pl.BlockSpec(memory_space=pl.ANY)] * 3,
        out_specs=pl.BlockSpec(memory_space=pl.ANY),
        out_shape=jax.ShapeDtypeStruct(out, BF16),
        scratch_shapes=[
            pltpu.VMEM((fcols, nfeat * rows_dev), BF16),
            pltpu.VMEM(out, BF16),
            pltpu.VMEM((fcols, 2 * hid), BF16),
            pltpu.SemaphoreType.DMA((parts,)),
            pltpu.SemaphoreType.DMA((parts,)),
            pltpu.SemaphoreType.DMA((2,)),
        ],
        name="pack",
        compiler_params=pltpu.CompilerParams(vmem_limit_bytes=60 << 20),
        cost_estimate=pl.CostEstimate(flops=0, bytes_accessed=3 << 20, transcendentals=0),
    )(place, feats, w_self, w_neigh)


def contract_rows(a, b):
    return lax.dot_general(a, b, (((0,), (0,)), ((), ())), preferred_element_type=F32)


def row_tile(ref, q, fcols):
    return ref[:, q * fcols : (q + 1) * fcols, :].reshape(ref.shape[0] * fcols, TILE)


def own_part(place, same_core, other_core, x_rows, bias, tiles):
    nx, nfeat, share, _ = same_core.shape
    hid = bias.shape[1]
    fcols = 2 * share

    def kernel(at, w0, w1, x_ref, b_ref, pre_ref, wn_ref, both):
        for k in range(nx):
            x = lax.bitwise_xor(lax.div(at[0], 2), k)
            lanes = pl.ds(pl.multiple_of(x * TILE, TILE), TILE)
            for r, ref in enumerate((w0, w1)):
                core = lax.bitwise_xor(lax.rem(at[0], 2), r)
                both[:, pl.ds(pl.multiple_of(core * share, share), share), lanes] = ref[k]
        ws = both[:, :, :hid].reshape(nfeat * fcols, hid)
        wn_ref[...] = both[:, :, hid:].reshape(nfeat * fcols, hid)
        for q in range(tiles):
            pre_ref[q] = contract_rows(row_tile(x_ref, q, fcols), ws) + b_ref[...]

    return pl.pallas_call(
        kernel,
        in_specs=[pl.BlockSpec(memory_space=pltpu.SMEM)] + in_vmem(4),
        out_specs=in_vmem(2),
        out_shape=[
            jax.ShapeDtypeStruct((tiles, TILE, hid), F32),
            jax.ShapeDtypeStruct((nfeat * fcols, hid), BF16),
        ],
        scratch_shapes=[pltpu.VMEM((nfeat, fcols, 2 * hid), BF16)],
        name="own_part",
        compiler_params=pltpu.CompilerParams(vmem_limit_bytes=16 << 20),
        cost_estimate=pl.CostEstimate(
            flops=2 * nfeat * fcols * tiles * TILE * hid, bytes_accessed=4 << 20, transcendentals=0
        ),
    )(place, same_core, other_core, x_rows, bias)


def layer(place, pre_own, a_rows, w_neigh, x_rows, upstream):
    nfeat = x_rows.shape[0]
    feats, hid = w_neigh.shape
    fcols = feats // nfeat
    rows = upstream.shape[0]
    tiles = rows // TILE
    halves = hid // TILE
    out_rows = halves * fcols + 8

    def kernel(at, pre, a_ref, wn, x_ref, up_ref, hid_ref, g_ref, deltas):
        gb = jnp.zeros((1, hid), F32)
        for q in range(tiles):
            here = slice(q * TILE, (q + 1) * TILE)
            v = pre[q] + contract_rows(row_tile(a_ref, q, fcols), wn[...])
            sq = v * v
            t = jnp.tanh(GELU_A * (v + GELU_B * sq * v))
            half = 0.5 * (1.0 + t)
            hid_ref[here, :] = (v * half).astype(BF16)
            slope = half + 0.5 * v * (1.0 - t * t) * (GELU_A * (1.0 + 3.0 * GELU_B * sq))
            delta = (up_ref[here, :].astype(F32) * slope).astype(BF16)
            deltas[here, :] = delta
            gb = gb + jnp.sum(delta.astype(F32), axis=0, keepdims=True)
        core = lax.rem(at[0], 2)
        for slot, ref in ((core, x_ref), (1 - core, a_ref)):
            left = jnp.concatenate([row_tile(ref, q, fcols) for q in range(tiles)], axis=1)
            grad = jnp.dot(left, deltas[...], preferred_element_type=F32).astype(BF16)
            for h in range(halves):
                g_ref[slot, :, h * fcols : (h + 1) * fcols, :] = grad[:, h * TILE : (h + 1) * TILE].reshape(
                    nfeat, fcols, TILE
                )
        high = gb.astype(BF16).astype(F32)
        mid = (gb - high).astype(BF16).astype(F32)
        low = gb - high - mid
        lines = [part[:, h * TILE : (h + 1) * TILE] for part in (high, mid, low) for h in range(halves)]
        lines = jnp.concatenate(lines + [jnp.zeros((8 - len(lines), TILE), F32)], axis=0).astype(BF16)
        g_ref[0, :, halves * fcols :, :] = jnp.broadcast_to(lines[None], (nfeat, 8, TILE))
        g_ref[1, :, halves * fcols :, :] = jnp.zeros((nfeat, 8, TILE), BF16)

    return pl.pallas_call(
        kernel,
        in_specs=[pl.BlockSpec(memory_space=pltpu.SMEM)] + in_vmem(5),
        out_specs=in_vmem(2),
        out_shape=[
            jax.ShapeDtypeStruct((rows, hid), BF16),
            jax.ShapeDtypeStruct((2, nfeat, out_rows, TILE), BF16),
        ],
        scratch_shapes=[pltpu.VMEM((rows, hid), BF16)],
        name="layer",
        compiler_params=pltpu.CompilerParams(vmem_limit_bytes=24 << 20),
        cost_estimate=pl.CostEstimate(
            flops=6 * feats * rows * hid, bytes_accessed=6 << 20, transcendentals=rows * hid
        ),
    )(place, pre_own, a_rows, w_neigh, x_rows, upstream)


def finish(place, mine, other, fcols):
    halves = (mine.shape[0] - 8) // fcols
    hid = halves * TILE

    def kernel(at, m_ref, o_ref, gs_ref, gn_ref, gb_ref):
        first = lax.rem(at[0], 2) == 0
        for h in range(halves):
            lanes, rows = slice(h * TILE, (h + 1) * TILE), slice(h * fcols, (h + 1) * fcols)
            gs_ref[:, lanes] = jnp.where(first, m_ref[rows], o_ref[rows])
            gn_ref[:, lanes] = jnp.where(first, o_ref[rows], m_ref[rows])
        both = m_ref[halves * fcols :] + o_ref[halves * fcols :]
        for h in range(halves):
            parts = [both[halves * p + h : halves * p + h + 1] for p in range(3)]
            gb_ref[:, h * TILE : (h + 1) * TILE] = parts[0] + parts[1] + parts[2]

    return pl.pallas_call(
        kernel,
        in_specs=[pl.BlockSpec(memory_space=pltpu.SMEM)] + in_vmem(2),
        out_specs=in_vmem(3),
        out_shape=[
            jax.ShapeDtypeStruct((fcols, hid), F32),
            jax.ShapeDtypeStruct((fcols, hid), F32),
            jax.ShapeDtypeStruct((1, hid), F32),
        ],
        name="finish",
        compiler_params=pltpu.CompilerParams(vmem_limit_bytes=8 << 20),
    )(place, mine, other)


def body(features_t, tile_weights, tile_dst, tile_src, tile_count, w_self, w_neigh, bias, grad_hidden):
    feats = features_t[0]
    fcols = feats.shape[0]
    nv = lax.axis_size("vgroup")
    nfeat = lax.axis_size("feat")
    rows_dev, hid = grad_hidden.shape
    tiles = rows_dev // TILE
    place = lax.axis_index("vgroup")[None].astype(jnp.int32)

    def direct(value, bits):
        return [lax.ppermute(value, "vgroup", [(a, a ^ bit) for a in range(nv)]) for bit in bits]

    with jax.named_scope("send_features"):
        outgoing = pack(place, feats, w_self, w_neigh, nfeat, rows_dev)
        x_rows = lax.all_to_all(outgoing, "feat", 0, 0, tiled=True)

    agg = aggregate(tile_dst[0], tile_src[0], tile_count, feats, tile_weights[0], nfeat)
    x_rows, agg = lax.optimization_barrier((x_rows, agg))
    with jax.named_scope("send_aggregated"):
        a_rows = lax.all_to_all(agg, "feat", 0, 0, tiled=True)

    with jax.named_scope("weights_over_vgroup"):
        part = x_rows[:, tiles * fcols :, :]
        other = lax.ppermute(part, "feat", [(a, a ^ 1) for a in range(nfeat)])
        even = lax.axis_index("feat") % 2 == 0
        piece = jnp.concatenate([jnp.where(even, part, other), jnp.where(even, other, part)], axis=1)
        near, side, far = direct(piece, (2, 6, 4))
        same_core = jnp.stack([piece, near, far, side])
        [other_core] = direct(same_core, (1,))

    pre_own, wn = own_part(place, same_core, other_core, x_rows, bias[None, :], tiles)
    hidden, grads = layer(place, pre_own, a_rows, wn, x_rows, grad_hidden)

    with jax.named_scope("reduce_grads"):
        [got] = direct(grads[1], (1,))
        pair = (grads[0].astype(F32) + got.astype(F32)).astype(BF16)
        arrived = lax.all_to_all(pair, "feat", 0, 0, tiled=True)
        total = jnp.sum(arrived.astype(F32), axis=0)
        total = sum(direct(total, (2, 6, 4)), total)
        [other] = direct(total, (1,))
        grad_self, grad_neigh, grad_bias = finish(place, total, other, fcols)
    return (hidden, grad_self, grad_neigh, grad_bias[0])


def solution(mesh):
    return jax.shard_map(
        body,
        mesh=mesh,
        in_specs=(
            P("vgroup", "feat", None),
            P("vgroup", None, None, None),
            P("vgroup", None),
            P("vgroup", None),
            P("vgroup"),
            P("feat", None),
            P("feat", None),
            P(),
            P(("vgroup", "feat"), None),
        ),
        out_specs=(P(("vgroup", "feat"), None), P("feat", None), P("feat", None), P()),
        check_vma=False,
    )
```
